512 devices in a mesh: tm: 32 (over z_lo, y), space: 16 (over z_hi, x, core).
Axes of the slice: x: 4, y: 4, z: 16 (z_hi: 2, z_lo: 8; z = z_hi * 8 + z_lo), core: 2. Of those that a mesh axis runs over, the one named last changes fastest.
Arguments:
- u_nodes: float32 [32, 3, 3, 64, 8, 128], P('tm', None, None, 'space'), may hold values from -4 to 4
Outputs:
- new_nodes: float32 [32, 3, 3, 64, 8, 128], P('tm', None, None, 'space')
The draws below stay inside these ranges and needn't reach their ends.
All inputs are finite; a program needn't handle non-finite values.
Results may differ from the reference program's by a relative error of at most 0.0003.
Values sent between devices are 32-bit elements; how exact they have to be, the bound alone decides.
No kernel may reach another device: no remote copies, remote signals or barrier semaphores. Data moves between devices by JAX's collectives and lax.ppermute only.
A program may use at most 64 MiB of HBM per device.

```python
import jax
import jax.numpy as jnp
from jax import lax

NX = 128
NY = 8
ITERS = 1
TIME_SLICES = 32
NZ = 64


def shard_levels(own_key, dims, pieces, low, high):
    def one(position, shards_of):
        draws = jax.random.uniform(jax.random.fold_in(jax.random.fold_in(own_key, 6), position), (shards_of,), jnp.float32, low / len(pieces), high / len(pieces))
        return jnp.repeat(jnp.exp(draws), dims[position] // shards_of).reshape((-1,) + (1,) * (len(dims) - position - 1))

    loudness = one(*pieces[0])
    for cut in pieces[1:]:
        loudness = loudness * one(*cut)
    return loudness


def normal_values(key, extent, deviation, limit, shards=(), kind=jnp.bfloat16):
    result = deviation * jax.random.normal(key, extent, jnp.float32)
    if shards:
        result = result * shard_levels(key, extent, shards, -0.22, 0.18)
    return jnp.clip(result, -limit, limit).astype(kind)


def setup_inputs(seed: int = 0) -> dict:
    splits = jax.random.split(jax.random.key(seed), 2)
    u_nodes = normal_values(splits[0], (TIME_SLICES, 3, 3, NZ, NY, NX), 0.6, 4.0, ((0, 32), (3, 16)), jnp.float32)
    return {"u_nodes": u_nodes}


STEP = 0.2
VISCOSITY = 0.1
FIRST_ROW = (5.0 / 24.0, 1.0 / 3.0, -1.0 / 24.0)
SECOND_ROW = (-1.0 / 24.0, 1.0 / 3.0, 5.0 / 24.0)


def tendency(padded, width, spacing, depth):
    middle = lax.slice_in_dim(padded, width, width + depth, axis=-3)
    upper = lax.slice_in_dim(padded, width + 1, width + 1 + depth, axis=-3)
    lower = lax.slice_in_dim(padded, width - 1, width - 1 + depth, axis=-3)
    north = jnp.roll(middle, -1, axis=-2)
    south = jnp.roll(middle, 1, axis=-2)
    east = jnp.roll(middle, -1, axis=-1)
    west = jnp.roll(middle, 1, axis=-1)
    vel_x = lax.slice_in_dim(middle, 0, 1, axis=-4)
    vel_y = lax.slice_in_dim(middle, 1, 2, axis=-4)
    vel_z = lax.slice_in_dim(middle, 2, 3, axis=-4)
    advect = vel_x * (east - west) + vel_y * (north - south) + vel_z * (upper - lower)
    diffuse = upper + lower + north + south + east + west - 6.0 * middle
    return diffuse * (VISCOSITY / (spacing * spacing)) - advect * (0.5 / spacing)


def zpad(field, width):
    return jnp.pad(field, [(0, 0)] * (field.ndim - 3) + [(width, width), (0, 0), (0, 0)])


def restrict(field):
    lead = field.shape[:-3]
    depth, rows, cols = field.shape[-3:]
    blocks = field.reshape(lead + (depth // 2, 2, rows // 2, 2, cols // 2, 2))
    return jnp.mean(blocks, axis=(-5, -3, -1))


def prolong(field):
    return jnp.repeat(jnp.repeat(jnp.repeat(field, 2, axis=-3), 2, axis=-2), 2, axis=-1)


def fine_section(nodes):
    f_all = tendency(zpad(nodes, 1), 1, 1.0, NZ)
    start = nodes[0]
    mid_value = start + STEP * (FIRST_ROW[0] * f_all[0] + FIRST_ROW[1] * f_all[1] + FIRST_ROW[2] * f_all[2])
    f_mid = tendency(zpad(mid_value, 1), 1, 1.0, NZ)
    end_value = mid_value + (0.5 * STEP * (f_mid - f_all[1]) + STEP * (SECOND_ROW[0] * f_all[0] + SECOND_ROW[1] * f_all[1] + SECOND_ROW[2] * f_all[2]))
    f_end = tendency(zpad(end_value, 1), 1, 1.0, NZ)
    integral = STEP * (f_all[0] / 6.0 + (2.0 / 3.0) * f_mid + f_end / 6.0)
    v_start = restrict(start)
    h_start = tendency(zpad(v_start, 1), 1, 2.0, NZ // 2)
    base = restrict(integral) - STEP * h_start
    return mid_value, end_value, v_start, restrict(end_value), base


def iterate(u_nodes):
    mids, ends, v_starts, v_ends, bases = lax.map(fine_section, u_nodes)
    count = u_nodes.shape[0]

    def link(prev_end, inputs):
        index, v_start, base = inputs
        w_start = jnp.where(index == 0, v_start, prev_end)
        w_end = w_start + (STEP * tendency(zpad(w_start, 1), 1, 2.0, NZ // 2) + base)
        return w_end, (w_start, w_end)

    _, (w_starts, w_ends) = lax.scan(link, jnp.zeros_like(v_starts[0]), (jnp.arange(count, dtype=jnp.int32), v_starts, bases))
    delta_start = w_starts - v_starts
    delta_end = w_ends - v_ends
    new_mid = mids + prolong(0.5 * (delta_start + delta_end))
    new_end = ends + prolong(delta_end)
    new_start = jnp.concatenate([u_nodes[0:1, 0], new_end[:-1]], axis=0)
    return jnp.stack([new_start, new_mid, new_end], axis=1)


def reference(u_nodes):
    nodes = u_nodes
    for turn in range(ITERS):
        nodes = iterate(nodes)
    return nodes
```

```python
import functools
import operator

import jax
import jax.numpy as jnp
from jax import lax
from jax.experimental import pallas as pl
from jax.experimental.pallas import tpu as pltpu
from jax.sharding import PartitionSpec as P

STEP = 0.2
VISCOSITY = 0.1
FIRST_ROW = (5.0 / 24.0, 1.0 / 3.0, -1.0 / 24.0)
SECOND_ROW = (-1.0 / 24.0, 1.0 / 3.0, 5.0 / 24.0)

GRAY = (0, 1, 3, 2)
WIDE = 3
PARAMS = pltpu.CompilerParams(vmem_limit_bytes=24 * 1024 * 1024)
GROUPS = 4
CORNERS = (8, 12, 16, 24)


def at_x(tile, shift):
    return pltpu.roll(tile, (-shift) % 128, 1)


def at_y(tile, shift):
    return pltpu.roll(tile, (-shift) % 8, 0)


def parities():
    row = lax.broadcasted_iota(jnp.int32, (8, 128), 0) & 1
    col = lax.broadcasted_iota(jnp.int32, (8, 128), 1) & 1
    return row, col


def swap_x(tile, odd_x):
    return jnp.where(odd_x, at_x(tile, -1), at_x(tile, 1))


def swap_y(tile, odd_y):
    return jnp.where(odd_y, at_y(tile, -1), at_y(tile, 1))


def rates(vel, upper, middle, lower, spacing, stride):
    north, south = at_y(middle, stride), at_y(middle, -stride)
    east, west = at_x(middle, stride), at_x(middle, -stride)
    advect = vel[0] * (east - west) + vel[1] * (north - south) + vel[2] * (upper - lower)
    diffuse = (upper + lower) + (north + south) + (east + west) - 6.0 * middle
    return diffuse * (VISCOSITY / (spacing * spacing)) - advect * (0.5 / spacing)


def tendency(planes, low, high, spacing, stride):
    out = [{} for _ in range(3)]
    for z in range(low, high):
        vel = [planes[c][z] for c in range(3)]
        for c in range(3):
            out[c][z] = rates(vel, planes[c][z + 1], planes[c][z], planes[c][z - 1], spacing, stride)
    return out


def restrict_pair(first, second, odd_y, odd_x):
    total = first + second
    total = total + swap_y(total, odd_y)
    total = total + swap_x(total, odd_x)
    return total * 0.125


def fine_kernel(near_ref, side_ref, nodes_ref, mid_ref, end_ref, start_c_ref, end_c_ref, packed_ref):
    here = lax.axis_index("space")
    last = lax.axis_size("space") - 1
    even = here % 2 == 0
    is_first = lax.axis_index("tm") == 0
    row, col = parities()
    odd_y, odd_x = row == 1, col == 1
    keep_low = here > 0
    keep_high = here < last
    def load(node):
        planes = [{} for _ in range(3)]
        for c in range(3):
            for z in range(-3, 7):
                if z < 0:
                    at = node, c, z + WIDE
                    planes[c][z] = jnp.where(even, side_ref[at], near_ref[at])
                elif z < 4:
                    planes[c][z] = nodes_ref[node, c, z]
                else:
                    at = node, c, z - 4
                    planes[c][z] = jnp.where(even, near_ref[at], side_ref[at])
        return planes

    def inside(tile, z):
        if z < 0:
            return jnp.where(keep_low, tile, 0.0)
        if z > 3:
            return jnp.where(keep_high, tile, 0.0)
        return tile

    start = load(0)
    f0 = tendency(start, -2, 6, 1.0, 1)
    f1 = tendency(load(1), -2, 6, 1.0, 1)
    f2 = tendency(load(2), -2, 6, 1.0, 1)
    mid = [{} for _ in range(3)]
    for c in range(3):
        for z in range(-2, 6):
            value = start[c][z] + STEP * (
                FIRST_ROW[0] * f0[c][z] + FIRST_ROW[1] * f1[c][z] + FIRST_ROW[2] * f2[c][z]
            )
            mid[c][z] = inside(value, z)
    f_mid = tendency(mid, -1, 5, 1.0, 1)
    end = [{} for _ in range(3)]
    for c in range(3):
        for z in range(-1, 5):
            value = mid[c][z] + (
                0.5 * STEP * (f_mid[c][z] - f1[c][z])
                + STEP * (SECOND_ROW[0] * f0[c][z] + SECOND_ROW[1] * f1[c][z] + SECOND_ROW[2] * f2[c][z])
            )
            end[c][z] = inside(value, z)
    f_end = tendency(end, 0, 4, 1.0, 1)
    coarse = [
        {k: restrict_pair(start[c][2 * k], start[c][2 * k + 1], odd_y, odd_x) for k in range(-1, 3)} for c in range(3)
    ]
    h_start = tendency(coarse, 0, 2, 2.0, 2)
    planes = []
    for c in range(3):
        for z in range(4):
            mid_ref[c, z] = mid[c][z]
            end_ref[c, z] = end[c][z]
        for k in range(2):
            start_c_ref[c, k] = coarse[c][k]
            end_c_ref[c, k] = restrict_pair(end[c][2 * k], end[c][2 * k + 1], odd_y, odd_x)
            integral = [
                STEP * (f0[c][z] / 6.0 + (2.0 / 3.0) * f_mid[c][z] + f_end[c][z] / 6.0) for z in (2 * k, 2 * k + 1)
            ]
            base = restrict_pair(integral[0], integral[1], odd_y, odd_x) - STEP * h_start[c][k]
            first_end = coarse[c][k] + (STEP * h_start[c][k] + base)
            planes.append(jnp.where(is_first, first_end, base))
    group = here // 4
    own = group ^ (group >> 1)
    place = (row * 2 + col) ^ own
    packed_ref[0] = jnp.where(
        place == 0, planes[0], jnp.where(place == 1, planes[1], jnp.where(place == 2, planes[2], planes[3]))
    )
    packed_ref[1] = jnp.where(place == 0, planes[4], jnp.where(place == 1, planes[5], 0.0))


def merge_kernel(own_ref, other_ref, column_ref):
    column_ref[0] = own_ref[0]
    column_ref[1] = other_ref[0]
    column_ref[2] = own_ref[1] + other_ref[1]


def spread_kernel(column_ref, passed_ref, copies_ref):
    tiles = column_ref[0], column_ref[1] + passed_ref[0], column_ref[2] + passed_ref[1]
    for i in range(copies_ref.shape[0]):
        for n in range(3):
            copies_ref[i, n] = tiles[n]


def unpacker(own_ref, other_ref, odd_y, odd_x, slot, core=None):
    here = lax.axis_index("space")
    half_z = here // 8

    def moved(tile, by):
        if by & 1:
            tile = swap_x(tile, odd_x)
        if by & 2:
            tile = swap_y(tile, odd_y)
        return tile

    def unpack(i):
        tiles = [[None] * 8 for _ in range(3)]
        for j in range(4):
            for half in range(2):
                sent = []
                for g in range(4):
                    slab = 4 * g + j
                    at = i * 4 + (slab % 8) // 2, 2 if half else (slab // 8) ^ half_z
                    if core is None:
                        sent.append(jnp.where(here % 2 == slab % 2, own_ref[at], other_ref[at]))
                    else:
                        sent.append(own_ref[at] if core == slab % 2 else other_ref[at])
                for q in range(4 if half == 0 else 2):
                    place = slot ^ q
                    merged = jnp.where(
                        place == GRAY[0],
                        sent[0],
                        jnp.where(place == GRAY[1], sent[1], jnp.where(place == GRAY[2], sent[2], sent[3])),
                    )
                    plane = 4 * half + q
                    tiles[plane // 2][2 * j + plane % 2] = moved(merged, q)
        return tiles

    return unpack


def chain_step(flat, base, slot):
    now = [list(flat[8 * c : 8 * c + 8]) for c in range(3)]
    planes = [{k: now[c][k] for k in range(8)} for c in range(3)]
    for c in range(3):
        top = now[c][0]
        planes[c][8] = jnp.where(
            slot == GRAY[0],
            at_x(top, 1),
            jnp.where(slot == GRAY[1], at_y(top, 1), jnp.where(slot == GRAY[2], at_x(top, -1), 0.0)),
        )
        low = now[c][7]
        planes[c][-1] = jnp.where(
            slot == GRAY[1],
            at_x(low, -1),
            jnp.where(slot == GRAY[2], at_y(low, -1), jnp.where(slot == GRAY[3], at_x(low, 1), 0.0)),
        )
    spread = STEP * VISCOSITY / 4.0
    after = []
    vel = [[(STEP * 0.25) * planes[c][k] for k in range(8)] for c in range(3)]
    for c in range(3):
        for k in range(8):
            middle, upper, lower = planes[c][k], planes[c][k + 1], planes[c][k - 1]
            north, south = at_y(middle, 2), at_y(middle, -2)
            east, west = at_x(middle, 2), at_x(middle, -2)
            around = (upper + lower) + (north + south) + (east + west)
            advect = vel[0][k] * (east - west) + vel[1][k] * (north - south) + vel[2][k] * (upper - lower)
            after.append((base[c][k] + (1.0 - 6.0 * spread) * middle) + (spread * around - advect))
    return tuple(after)


def flat_tiles(tiles):
    return tuple(tile for row in tiles for tile in row)


def unpack_kernel(count, own_ref, other_ref, base_ref):
    row, col = parities()
    unpack = unpacker(own_ref, other_ref, row == 1, col == 1, row * 2 + col)
    for i in range(count):
        for n, tile in enumerate(flat_tiles(unpack(i))):
            base_ref[i, n] = tile


def stored(base_ref, i):
    return [[base_ref[i, 8 * c + k] for k in range(8)] for c in range(3)]


def runs_wave(wave, count):
    return (lax.axis_index("tm") // count == wave) & (lax.axis_index("space") % 2 == 0)


def first_wave_kernel(count, own_ref, other_ref, out_ref):
    row, col = parities()
    slot = row * 2 + col
    unpack = unpacker(own_ref, other_ref, row == 1, col == 1, slot, 0)

    @pl.when(runs_wave(0, count))
    def _():
        state = flat_tiles(unpack(0))
        for i in range(1, count):
            state = chain_step(state, unpack(i), slot)
        for n in range(24):
            out_ref[n] = state[n]


def wave_kernel(wave, count, base_ref, state_ref, out_ref):
    row, col = parities()
    slot = row * 2 + col

    @pl.when(runs_wave(wave, count))
    def _():
        state = tuple(state_ref[n] for n in range(24))
        for i in range(count):
            state = chain_step(state, stored(base_ref, i), slot)
        for n in range(24):
            out_ref[n] = state[n]


def last_kernel(
    count, base_ref, state_ref, given_ref, late_ref, nodes_ref, mid_ref, end_ref, prev_ref, edge_ref,
    start_c_ref, end_c_ref, out_ref, states,
):
    here = lax.axis_index("space")
    slice_id = lax.axis_index("tm")
    row, col = parities()
    odd_y, odd_x = row == 1, col == 1
    slot = row * 2 + col
    own = slice_id % count
    in_first = slice_id // count == 0
    is_last = slice_id // count == GROUPS - 1
    at_corner = functools.reduce(operator.or_, [slice_id == i for i in CORNERS])

    def keep(i, flat):
        for n in range(24):
            states[i, n] = flat[n]

    from_own = here % 2 == 0
    state = tuple(
        jnp.where(from_own, state_ref[n], jnp.where(is_last, late_ref[n], given_ref[n])) for n in range(24)
    )
    keep(0, state)
    for i in range(count):
        base = stored(base_ref, i)
        state = chain_step(state, base, slot)
        if i == 0:
            state = tuple(jnp.where(in_first, b, after) for b, after in zip(flat_tiles(base), state))
        keep(i + 1, state)

    group = here // 4
    code = group ^ (group >> 1)
    own_y, own_x = code >> 1, code & 1
    base_k = 2 * (here % 4)

    def spread(tile):
        tile = jnp.where(row == own_y, tile, swap_y(tile, odd_y))
        return jnp.where(col == own_x, tile, swap_x(tile, odd_x))

    is_first = slice_id == 0
    for c in range(3):
        for k in range(2):
            w_end = spread(states[own + 1, 8 * c + base_k + k])
            v_start = start_c_ref[c, k]
            w_start = jnp.where(is_first, v_start, spread(states[own, 8 * c + base_k + k]))
            delta_start = w_start - v_start
            delta_end = w_end - end_c_ref[c, k]
            half = 0.5 * (delta_start + delta_end)
            handed = [jnp.where(at_corner, edge_ref[c, 2 * k + i], prev_ref[c, 2 * k + i]) for i in range(2)]
            delta_prev = w_start - restrict_pair(handed[0], handed[1], odd_y, odd_x)
            for i in range(2):
                z = 2 * k + i
                out_ref[0, 0, c, z] = jnp.where(is_first, nodes_ref[0, c, z], handed[i] + delta_prev)
                out_ref[0, 1, c, z] = mid_ref[c, z] + half
                out_ref[0, 2, c, z] = end_ref[c, z] + delta_end


def vmem(count):
    return [pl.BlockSpec(memory_space=pltpu.VMEM)] * count


def local(u_nodes):
    nodes = u_nodes[0]
    depth = nodes.shape[2]
    slabs = lax.axis_size("space")
    slices = lax.axis_size("tm")
    tile = nodes.shape[3:]
    shape = lambda *lead: jax.ShapeDtypeStruct(lead + tile, jnp.float32)
    both = ("tm", "space")
    middle = slabs // 2
    even = lax.axis_index("space") % 2 == 0
    top, bottom = nodes[:, :, depth - WIDE :], nodes[:, :, :WIDE]

    def swaps(pairs):
        return [(i, j) for i, j in pairs] + [(j, i) for i, j in pairs]

    to_side = jnp.where(even, bottom, top)
    side = lax.ppermute(to_side, "space", swaps([(i, i + 1) for i in range(1, slabs - 1, 2)]))
    near = lax.ppermute(jnp.where(even, top, bottom), "space", swaps([(i, i + 1) for i in range(0, slabs, 2)]))
    mid, end, start_c, end_c, packed = pl.pallas_call(
        fine_kernel,
        out_shape=[shape(3, 4), shape(3, 4), shape(3, 2), shape(3, 2), shape(2)],
        in_specs=vmem(3),
        out_specs=vmem(5),
        compiler_params=PARAMS,
        name="fine",
    )(near, side, nodes)
    across = lax.ppermute(packed, "space", [(i, (i + middle) % slabs) for i in range(1, slabs)])
    beside = lax.ppermute(packed, "space", [(0, middle + 1)])
    column = pl.pallas_call(
        merge_kernel, out_shape=shape(3), in_specs=vmem(2), out_specs=vmem(1)[0], compiler_params=PARAMS, name="merge"
    )(packed, across)
    column, beside = lax.optimization_barrier((column, beside))
    passed = lax.ppermute(beside, "space", [(middle + 1, middle)])
    copies = pl.pallas_call(
        spread_kernel,
        out_shape=shape(32, 3),
        in_specs=vmem(2),
        out_specs=vmem(1)[0],
        compiler_params=PARAMS,
        name="spread",
    )(column, passed)

    device = lambda zl, y, zh, x, core: (zl * 4 + y) * slabs + zh * 8 + x * 2 + core
    layers = [
        [device(2 * g + zl, y, zh, x, core) for zl in range(2) for y in range(4) for x in range(4)]
        for g in range(GROUPS)
        for zh in range(2)
        for core in range(2)
    ]
    own = lax.all_to_all(copies, both, 0, 0, axis_index_groups=layers)
    edge = lax.ppermute(end, "tm", [(i - 1, i) for i in CORNERS])
    own, edge = lax.optimization_barrier((own, edge))
    other = lax.ppermute(own, "space", swaps([(i, i + 1) for i in range(0, slabs, 2)]))
    count = slices // GROUPS

    def cores(groups):
        return [((g * count + i) * slabs + s) for g in groups for i in range(count) for s in range(0, slabs, 2)]

    after = pl.pallas_call(
        functools.partial(first_wave_kernel, count),
        out_shape=shape(24),
        in_specs=vmem(2),
        out_specs=vmem(1)[0],
        compiler_params=PARAMS,
        name="wave",
    )(own, other)
    own, after = lax.optimization_barrier((own, after))
    bases = pl.pallas_call(
        functools.partial(unpack_kernel, count),
        out_shape=shape(count, 24),
        in_specs=vmem(2),
        out_specs=vmem(1)[0],
        compiler_params=PARAMS,
        cost_estimate=pl.CostEstimate(flops=10_000_000, bytes_accessed=10_000_000, transcendentals=0),
        name="unpack",
    )(own, other)
    state = lax.ppermute(after, both, [(i, i + count * slabs) for i in cores([0])])
    for wave in range(1, GROUPS - 1):
        after = pl.pallas_call(
            functools.partial(wave_kernel, wave, count),
            out_shape=shape(24),
            in_specs=vmem(2),
            out_specs=vmem(1)[0],
            compiler_params=PARAMS,
            name="wave",
        )(bases, state)
        early, after = lax.optimization_barrier((state, after))
        if wave == 1:
            handed, after = lax.optimization_barrier((end, after))
            prev = lax.ppermute(handed, "tm", [(i, i + 1) for i in range(slices - 1) if i + 1 not in CORNERS])
        moved = lax.ppermute(after, both, [(i, i + count * slabs) for i in cores([wave])])
        if wave == 1:
            prev, moved = lax.optimization_barrier((prev, moved))
        state = moved + early
    late = lax.ppermute(after, both, [(i, i + count * slabs + 1) for i in cores([GROUPS - 2])])
    given = lax.ppermute(early, both, [(i, i + 1) for i in cores(range(1, GROUPS - 1))])
    return pl.pallas_call(
        functools.partial(last_kernel, count),
        out_shape=shape(1, 3, 3, 4),
        in_specs=vmem(11),
        out_specs=vmem(1)[0],
        scratch_shapes=[pltpu.VMEM((count + 1, 24) + tile, jnp.float32)],
        compiler_params=PARAMS,
        name="last",
    )(bases, state, given, late, nodes, mid, end, prev, edge, start_c, end_c)


def solution(mesh):
    return jax.shard_map(
        local,
        mesh=mesh,
        in_specs=(P("tm", None, None, "space", None, None),),
        out_specs=P("tm", None, None, "space", None, None),
        check_vma=False,
    )
```

```python
import functools
import operator

import jax
import jax.numpy as jnp
from jax import lax
from jax.experimental import pallas as pl
from jax.experimental.pallas import tpu as pltpu
from jax.sharding import PartitionSpec as P

STEP = 0.2
VISCOSITY = 0.1
FIRST_ROW = (5.0 / 24.0, 1.0 / 3.0, -1.0 / 24.0)
SECOND_ROW = (-1.0 / 24.0, 1.0 / 3.0, 5.0 / 24.0)

GRAY = (0, 1, 3, 2)
WIDE = 3
PARAMS = pltpu.CompilerParams(vmem_limit_bytes=24 * 1024 * 1024)
GROUPS = 4
CORNERS = (8, 12, 16, 24)


def at_x(tile, shift):
    return pltpu.roll(tile, (-shift) % 128, 1)


def at_y(tile, shift):
    return pltpu.roll(tile, (-shift) % 8, 0)


def parities():
    row = lax.broadcasted_iota(jnp.int32, (8, 128), 0) & 1
    col = lax.broadcasted_iota(jnp.int32, (8, 128), 1) & 1
    return row, col


def swap_x(tile, odd_x):
    return jnp.where(odd_x, at_x(tile, -1), at_x(tile, 1))


def swap_y(tile, odd_y):
    return jnp.where(odd_y, at_y(tile, -1), at_y(tile, 1))


def rates(vel, upper, middle, lower, spacing, stride):
    north, south = at_y(middle, stride), at_y(middle, -stride)
    east, west = at_x(middle, stride), at_x(middle, -stride)
    advect = vel[0] * (east - west) + vel[1] * (north - south) + vel[2] * (upper - lower)
    diffuse = (upper + lower) + (north + south) + (east + west) - 6.0 * middle
    return diffuse * (VISCOSITY / (spacing * spacing)) - advect * (0.5 / spacing)


def tendency(planes, low, high, spacing, stride):
    out = [{} for _ in range(3)]
    for z in range(low, high):
        vel = [planes[c][z] for c in range(3)]
        for c in range(3):
            out[c][z] = rates(vel, planes[c][z + 1], planes[c][z], planes[c][z - 1], spacing, stride)
    return out


def restrict_pair(first, second, odd_y, odd_x):
    total = first + second
    total = total + swap_y(total, odd_y)
    total = total + swap_x(total, odd_x)
    return total * 0.125


def fine_kernel(near_ref, side_ref, nodes_ref, mid_ref, end_ref, start_c_ref, end_c_ref, packed_ref, again_ref):
    here = lax.axis_index("space")
    last = lax.axis_size("space") - 1
    even = here % 2 == 0
    is_first = lax.axis_index("tm") == 0
    row, col = parities()
    odd_y, odd_x = row == 1, col == 1
    keep_low = here > 0
    keep_high = here < last
    def load(node):
        planes = [{} for _ in range(3)]
        for c in range(3):
            for z in range(-3, 7):
                if z < 0:
                    at = node, c, z + WIDE
                    planes[c][z] = jnp.where(even, side_ref[at], near_ref[at])
                elif z < 4:
                    planes[c][z] = nodes_ref[node, c, z]
                else:
                    at = node, c, z - 4
                    planes[c][z] = jnp.where(even, near_ref[at], side_ref[at])
        return planes

    def inside(tile, z):
        if z < 0:
            return jnp.where(keep_low, tile, 0.0)
        if z > 3:
            return jnp.where(keep_high, tile, 0.0)
        return tile

    start = load(0)
    f0 = tendency(start, -2, 6, 1.0, 1)
    f1 = tendency(load(1), -2, 6, 1.0, 1)
    f2 = tendency(load(2), -2, 6, 1.0, 1)
    mid = [{} for _ in range(3)]
    for c in range(3):
        for z in range(-2, 6):
            value = start[c][z] + STEP * (
                FIRST_ROW[0] * f0[c][z] + FIRST_ROW[1] * f1[c][z] + FIRST_ROW[2] * f2[c][z]
            )
            mid[c][z] = inside(value, z)
    f_mid = tendency(mid, -1, 5, 1.0, 1)
    end = [{} for _ in range(3)]
    for c in range(3):
        for z in range(-1, 5):
            value = mid[c][z] + (
                0.5 * STEP * (f_mid[c][z] - f1[c][z])
                + STEP * (SECOND_ROW[0] * f0[c][z] + SECOND_ROW[1] * f1[c][z] + SECOND_ROW[2] * f2[c][z])
            )
            end[c][z] = inside(value, z)
    f_end = tendency(end, 0, 4, 1.0, 1)
    coarse = [
        {k: restrict_pair(start[c][2 * k], start[c][2 * k + 1], odd_y, odd_x) for k in range(-1, 3)} for c in range(3)
    ]
    h_start = tendency(coarse, 0, 2, 2.0, 2)
    planes = []
    for c in range(3):
        for z in range(4):
            mid_ref[c, z] = mid[c][z]
            end_ref[c, z] = end[c][z]
        for k in range(2):
            start_c_ref[c, k] = coarse[c][k]
            end_c_ref[c, k] = restrict_pair(end[c][2 * k], end[c][2 * k + 1], odd_y, odd_x)
            integral = [
                STEP * (f0[c][z] / 6.0 + (2.0 / 3.0) * f_mid[c][z] + f_end[c][z] / 6.0) for z in (2 * k, 2 * k + 1)
            ]
            base = restrict_pair(integral[0], integral[1], odd_y, odd_x) - STEP * h_start[c][k]
            first_end = coarse[c][k] + (STEP * h_start[c][k] + base)
            planes.append(jnp.where(is_first, first_end, base))
    group = here // 4
    own = group ^ (group >> 1)
    place = (row * 2 + col) ^ own
    packed_ref[0] = jnp.where(
        place == 0, planes[0], jnp.where(place == 1, planes[1], jnp.where(place == 2, planes[2], planes[3]))
    )
    packed_ref[1] = jnp.where(place == 0, planes[4], jnp.where(place == 1, planes[5], 0.0))
    for n in range(2, packed_ref.shape[0]):
        packed_ref[n] = jnp.zeros((8, 128), jnp.float32)
    again_ref[0] = packed_ref[0]
    again_ref[1] = packed_ref[1]


def spread_kernel(own_ref, across_ref, passed_ref, copies_ref):
    other = [across_ref[n] + passed_ref[n] for n in range(2)]
    tiles = own_ref[0], other[0], own_ref[1] + other[1]
    for i in range(copies_ref.shape[0]):
        for n in range(3):
            copies_ref[i, n] = tiles[n]


def unpacker(own_ref, other_ref, odd_y, odd_x, slot, core=None):
    here = lax.axis_index("space")
    half_z = here // 8

    def moved(tile, by):
        if by & 1:
            tile = swap_x(tile, odd_x)
        if by & 2:
            tile = swap_y(tile, odd_y)
        return tile

    def unpack(i):
        tiles = [[None] * 8 for _ in range(3)]
        for j in range(4):
            for half in range(2):
                sent = []
                for g in range(4):
                    slab = 4 * g + j
                    at = i * 4 + (slab % 8) // 2, 2 if half else (slab // 8) ^ half_z
                    if core is None:
                        sent.append(jnp.where(here % 2 == slab % 2, own_ref[at], other_ref[at]))
                    else:
                        sent.append(own_ref[at] if core == slab % 2 else other_ref[at])
                for q in range(4 if half == 0 else 2):
                    place = slot ^ q
                    merged = jnp.where(
                        place == GRAY[0],
                        sent[0],
                        jnp.where(place == GRAY[1], sent[1], jnp.where(place == GRAY[2], sent[2], sent[3])),
                    )
                    plane = 4 * half + q
                    tiles[plane // 2][2 * j + plane % 2] = moved(merged, q)
        return tiles

    return unpack


def chain_step(flat, base, slot):
    now = [list(flat[8 * c : 8 * c + 8]) for c in range(3)]
    planes = [{k: now[c][k] for k in range(8)} for c in range(3)]
    for c in range(3):
        top = now[c][0]
        planes[c][8] = jnp.where(
            slot == GRAY[0],
            at_x(top, 1),
            jnp.where(slot == GRAY[1], at_y(top, 1), jnp.where(slot == GRAY[2], at_x(top, -1), 0.0)),
        )
        low = now[c][7]
        planes[c][-1] = jnp.where(
            slot == GRAY[1],
            at_x(low, -1),
            jnp.where(slot == GRAY[2], at_y(low, -1), jnp.where(slot == GRAY[3], at_x(low, 1), 0.0)),
        )
    spread = STEP * VISCOSITY / 4.0
    after = []
    vel = [[(STEP * 0.25) * planes[c][k] for k in range(8)] for c in range(3)]
    for c in range(3):
        for k in range(8):
            middle, upper, lower = planes[c][k], planes[c][k + 1], planes[c][k - 1]
            north, south = at_y(middle, 2), at_y(middle, -2)
            east, west = at_x(middle, 2), at_x(middle, -2)
            around = (upper + lower) + (north + south) + (east + west)
            advect = vel[0][k] * (east - west) + vel[1][k] * (north - south) + vel[2][k] * (upper - lower)
            after.append((base[c][k] + (1.0 - 6.0 * spread) * middle) + (spread * around - advect))
    return tuple(after)


def flat_tiles(tiles):
    return tuple(tile for row in tiles for tile in row)


def unpack_kernel(count, own_ref, other_ref, base_ref):
    row, col = parities()
    unpack = unpacker(own_ref, other_ref, row == 1, col == 1, row * 2 + col)
    for i in range(count):
        for n, tile in enumerate(flat_tiles(unpack(i))):
            base_ref[i, n] = tile


def stored(base_ref, i):
    return [[base_ref[i, 8 * c + k] for k in range(8)] for c in range(3)]


def runs_wave(wave, count):
    return (lax.axis_index("tm") // count == wave) & (lax.axis_index("space") % 2 == 0)


def first_wave_kernel(count, own_ref, other_ref, out_ref):
    row, col = parities()
    slot = row * 2 + col
    unpack = unpacker(own_ref, other_ref, row == 1, col == 1, slot, 0)

    @pl.when(runs_wave(0, count))
    def _():
        state = flat_tiles(unpack(0))
        for i in range(1, count):
            state = chain_step(state, unpack(i), slot)
        for n in range(24):
            out_ref[n] = state[n]


def wave_kernel(wave, count, base_ref, state_ref, out_ref):
    row, col = parities()
    slot = row * 2 + col

    @pl.when(runs_wave(wave, count))
    def _():
        state = tuple(state_ref[n] for n in range(24))
        for i in range(count):
            state = chain_step(state, stored(base_ref, i), slot)
        for n in range(24):
            out_ref[n] = state[n]


def last_kernel(
    count, base_ref, state_ref, given_ref, late_ref, nodes_ref, mid_ref, end_ref, prev_ref, edge_ref,
    start_c_ref, end_c_ref, out_ref, states,
):
    here = lax.axis_index("space")
    slice_id = lax.axis_index("tm")
    row, col = parities()
    odd_y, odd_x = row == 1, col == 1
    slot = row * 2 + col
    own = slice_id % count
    in_first = slice_id // count == 0
    is_last = slice_id // count == GROUPS - 1
    at_corner = functools.reduce(operator.or_, [slice_id == i for i in CORNERS])

    def keep(i, flat):
        for n in range(24):
            states[i, n] = flat[n]

    from_own = here % 2 == 0
    state = tuple(
        jnp.where(from_own, state_ref[n], jnp.where(is_last, late_ref[n], given_ref[n])) for n in range(24)
    )
    keep(0, state)
    for i in range(count):
        base = stored(base_ref, i)
        state = chain_step(state, base, slot)
        if i == 0:
            state = tuple(jnp.where(in_first, b, after) for b, after in zip(flat_tiles(base), state))
        keep(i + 1, state)

    group = here // 4
    code = group ^ (group >> 1)
    own_y, own_x = code >> 1, code & 1
    base_k = 2 * (here % 4)

    def spread(tile):
        tile = jnp.where(row == own_y, tile, swap_y(tile, odd_y))
        return jnp.where(col == own_x, tile, swap_x(tile, odd_x))

    is_first = slice_id == 0
    for c in range(3):
        for k in range(2):
            w_end = spread(states[own + 1, 8 * c + base_k + k])
            v_start = start_c_ref[c, k]
            w_start = jnp.where(is_first, v_start, spread(states[own, 8 * c + base_k + k]))
            delta_start = w_start - v_start
            delta_end = w_end - end_c_ref[c, k]
            half = 0.5 * (delta_start + delta_end)
            handed = [jnp.where(at_corner, edge_ref[c, 2 * k + i], prev_ref[c, 2 * k + i]) for i in range(2)]
            delta_prev = w_start - restrict_pair(handed[0], handed[1], odd_y, odd_x)
            for i in range(2):
                z = 2 * k + i
                out_ref[0, 0, c, z] = jnp.where(is_first, nodes_ref[0, c, z], handed[i] + delta_prev)
                out_ref[0, 1, c, z] = mid_ref[c, z] + half
                out_ref[0, 2, c, z] = end_ref[c, z] + delta_end


def vmem(count):
    return [pl.BlockSpec(memory_space=pltpu.VMEM)] * count


def local(u_nodes):
    nodes = u_nodes[0]
    depth = nodes.shape[2]
    slabs = lax.axis_size("space")
    slices = lax.axis_size("tm")
    tile = nodes.shape[3:]
    shape = lambda *lead: jax.ShapeDtypeStruct(lead + tile, jnp.float32)
    both = ("tm", "space")
    middle = slabs // 2
    even = lax.axis_index("space") % 2 == 0
    top, bottom = nodes[:, :, depth - WIDE :], nodes[:, :, :WIDE]

    def swaps(pairs):
        return [(i, j) for i, j in pairs] + [(j, i) for i, j in pairs]

    to_side = jnp.where(even, bottom, top)
    side = lax.ppermute(to_side, "space", swaps([(i, i + 1) for i in range(1, slabs - 1, 2)]))
    near = lax.ppermute(jnp.where(even, top, bottom), "space", swaps([(i, i + 1) for i in range(0, slabs, 2)]))
    mid, end, start_c, end_c, packed, again = pl.pallas_call(
        fine_kernel,
        out_shape=[shape(3, 4), shape(3, 4), shape(3, 2), shape(3, 2), shape(4), shape(2)],
        in_specs=vmem(3),
        out_specs=vmem(6),
        compiler_params=PARAMS,
        name="fine",
    )(near, side, nodes)
    across = lax.ppermute(packed, "space", [(i, (i + middle) % slabs) for i in range(1, slabs)])
    beside = lax.ppermute(again, "space", [(0, middle + 1)])
    passed = lax.ppermute(beside, "space", [(middle + 1, middle)])
    copies = pl.pallas_call(
        spread_kernel,
        out_shape=shape(32, 3),
        in_specs=vmem(3),
        out_specs=vmem(1)[0],
        compiler_params=PARAMS,
        name="spread",
    )(packed, across, passed)

    device = lambda zl, y, zh, x, core: (zl * 4 + y) * slabs + zh * 8 + x * 2 + core
    layers = [
        [device(2 * g + zl, y, zh, x, core) for zl in range(2) for y in range(4) for x in range(4)]
        for g in range(GROUPS)
        for zh in range(2)
        for core in range(2)
    ]
    own = lax.all_to_all(copies, both, 0, 0, axis_index_groups=layers)
    edge = lax.ppermute(end, "tm", [(i - 1, i) for i in CORNERS])
    own, edge = lax.optimization_barrier((own, edge))
    other = lax.ppermute(own, "space", swaps([(i, i + 1) for i in range(0, slabs, 2)]))
    count = slices // GROUPS

    def cores(groups):
        return [((g * count + i) * slabs + s) for g in groups for i in range(count) for s in range(0, slabs, 2)]

    after = pl.pallas_call(
        functools.partial(first_wave_kernel, count),
        out_shape=shape(24),
        in_specs=vmem(2),
        out_specs=vmem(1)[0],
        compiler_params=PARAMS,
        name="wave",
    )(own, other)
    own, after = lax.optimization_barrier((own, after))
    bases = pl.pallas_call(
        functools.partial(unpack_kernel, count),
        out_shape=shape(count, 24),
        in_specs=vmem(2),
        out_specs=vmem(1)[0],
        compiler_params=PARAMS,
        cost_estimate=pl.CostEstimate(flops=10_000_000, bytes_accessed=10_000_000, transcendentals=0),
        name="unpack",
    )(own, other)
    state = lax.ppermute(after, both, [(i, i + count * slabs) for i in cores([0])])
    for wave in range(1, GROUPS - 1):
        after = pl.pallas_call(
            functools.partial(wave_kernel, wave, count),
            out_shape=shape(24),
            in_specs=vmem(2),
            out_specs=vmem(1)[0],
            compiler_params=PARAMS,
            name="wave",
        )(bases, state)
        early, after = lax.optimization_barrier((state, after))
        if wave == 1:
            handed, after = lax.optimization_barrier((end, after))
            prev = lax.ppermute(handed, "tm", [(i, i + 1) for i in range(slices - 1) if i + 1 not in CORNERS])
        moved = lax.ppermute(after, both, [(i, i + count * slabs) for i in cores([wave])])
        if wave == 1:
            prev, moved = lax.optimization_barrier((prev, moved))
        state = moved + early
    late = lax.ppermute(after, both, [(i, i + count * slabs + 1) for i in cores([GROUPS - 2])])
    given = lax.ppermute(early, both, [(i, i + 1) for i in cores(range(1, GROUPS - 1))])
    return pl.pallas_call(
        functools.partial(last_kernel, count),
        out_shape=shape(1, 3, 3, 4),
        in_specs=vmem(11),
        out_specs=vmem(1)[0],
        scratch_shapes=[pltpu.VMEM((count + 1, 24) + tile, jnp.float32)],
        compiler_params=PARAMS,
        name="last",
    )(bases, state, given, late, nodes, mid, end, prev, edge, start_c, end_c)


def solution(mesh):
    return jax.shard_map(
        local,
        mesh=mesh,
        in_specs=(P("tm", None, None, "space", None, None),),
        out_specs=P("tm", None, None, "space", None, None),
        check_vma=False,
    )
```

```python
import functools
import operator

import jax
import jax.numpy as jnp
from jax import lax
from jax.experimental import pallas as pl
from jax.experimental.pallas import tpu as pltpu
from jax.sharding import PartitionSpec as P

STEP = 0.2
VISCOSITY = 0.1
FIRST_ROW = (5.0 / 24.0, 1.0 / 3.0, -1.0 / 24.0)
SECOND_ROW = (-1.0 / 24.0, 1.0 / 3.0, 5.0 / 24.0)

GRAY = (0, 1, 3, 2)
WIDE = 3
PARAMS = pltpu.CompilerParams(vmem_limit_bytes=24 * 1024 * 1024)
GROUPS = 4
CORNERS = (8, 12, 16, 24)


def at_x(tile, shift):
    return pltpu.roll(tile, (-shift) % 128, 1)


def at_y(tile, shift):
    return pltpu.roll(tile, (-shift) % 8, 0)


def parities():
    row = lax.broadcasted_iota(jnp.int32, (8, 128), 0) & 1
    col = lax.broadcasted_iota(jnp.int32, (8, 128), 1) & 1
    return row, col


def swap_x(tile, odd_x):
    return jnp.where(odd_x, at_x(tile, -1), at_x(tile, 1))


def swap_y(tile, odd_y):
    return jnp.where(odd_y, at_y(tile, -1), at_y(tile, 1))


def rates(vel, upper, middle, lower, spacing, stride):
    north, south = at_y(middle, stride), at_y(middle, -stride)
    east, west = at_x(middle, stride), at_x(middle, -stride)
    advect = vel[0] * (east - west) + vel[1] * (north - south) + vel[2] * (upper - lower)
    diffuse = (upper + lower) + (north + south) + (east + west) - 6.0 * middle
    return diffuse * (VISCOSITY / (spacing * spacing)) - advect * (0.5 / spacing)


def tendency(planes, low, high, spacing, stride):
    out = [{} for _ in range(3)]
    for z in range(low, high):
        vel = [planes[c][z] for c in range(3)]
        for c in range(3):
            out[c][z] = rates(vel, planes[c][z + 1], planes[c][z], planes[c][z - 1], spacing, stride)
    return out


def restrict_pair(first, second, odd_y, odd_x):
    total = first + second
    total = total + swap_y(total, odd_y)
    total = total + swap_x(total, odd_x)
    return total * 0.125


def fine_kernel(near_ref, side_ref, nodes_ref, mid_ref, end_ref, start_c_ref, end_c_ref, packed_ref, again_ref):
    here = lax.axis_index("space")
    last = lax.axis_size("space") - 1
    even = here % 2 == 0
    is_first = lax.axis_index("tm") == 0
    row, col = parities()
    odd_y, odd_x = row == 1, col == 1
    keep_low = here > 0
    keep_high = here < last
    def load(node):
        planes = [{} for _ in range(3)]
        for c in range(3):
            for z in range(-3, 7):
                if z < 0:
                    at = node, c, z + WIDE
                    planes[c][z] = jnp.where(even, side_ref[at], near_ref[at])
                elif z < 4:
                    planes[c][z] = nodes_ref[node, c, z]
                else:
                    at = node, c, z - 4
                    planes[c][z] = jnp.where(even, near_ref[at], side_ref[at])
        return planes

    def inside(tile, z):
        if z < 0:
            return jnp.where(keep_low, tile, 0.0)
        if z > 3:
            return jnp.where(keep_high, tile, 0.0)
        return tile

    start = load(0)
    f0 = tendency(start, -2, 6, 1.0, 1)
    f1 = tendency(load(1), -2, 6, 1.0, 1)
    f2 = tendency(load(2), -2, 6, 1.0, 1)
    mid = [{} for _ in range(3)]
    for c in range(3):
        for z in range(-2, 6):
            value = start[c][z] + STEP * (
                FIRST_ROW[0] * f0[c][z] + FIRST_ROW[1] * f1[c][z] + FIRST_ROW[2] * f2[c][z]
            )
            mid[c][z] = inside(value, z)
    f_mid = tendency(mid, -1, 5, 1.0, 1)
    end = [{} for _ in range(3)]
    for c in range(3):
        for z in range(-1, 5):
            value = mid[c][z] + (
                0.5 * STEP * (f_mid[c][z] - f1[c][z])
                + STEP * (SECOND_ROW[0] * f0[c][z] + SECOND_ROW[1] * f1[c][z] + SECOND_ROW[2] * f2[c][z])
            )
            end[c][z] = inside(value, z)
    f_end = tendency(end, 0, 4, 1.0, 1)
    coarse = [
        {k: restrict_pair(start[c][2 * k], start[c][2 * k + 1], odd_y, odd_x) for k in range(-1, 3)} for c in range(3)
    ]
    h_start = tendency(coarse, 0, 2, 2.0, 2)
    planes = []
    for c in range(3):
        for z in range(4):
            mid_ref[c, z] = mid[c][z]
            end_ref[c, z] = end[c][z]
        for k in range(2):
            start_c_ref[c, k] = coarse[c][k]
            end_c_ref[c, k] = restrict_pair(end[c][2 * k], end[c][2 * k + 1], odd_y, odd_x)
            integral = [
                STEP * (f0[c][z] / 6.0 + (2.0 / 3.0) * f_mid[c][z] + f_end[c][z] / 6.0) for z in (2 * k, 2 * k + 1)
            ]
            base = restrict_pair(integral[0], integral[1], odd_y, odd_x) - STEP * h_start[c][k]
            first_end = coarse[c][k] + (STEP * h_start[c][k] + base)
            planes.append(jnp.where(is_first, first_end, base))
    group = here // 4
    own = group ^ (group >> 1)
    place = (row * 2 + col) ^ own
    packed_ref[0] = jnp.where(
        place == 0, planes[0], jnp.where(place == 1, planes[1], jnp.where(place == 2, planes[2], planes[3]))
    )
    packed_ref[1] = jnp.where(place == 0, planes[4], jnp.where(place == 1, planes[5], 0.0))
    for n in range(2, packed_ref.shape[0]):
        packed_ref[n] = jnp.zeros((8, 128), jnp.float32)
    again_ref[0] = packed_ref[0]
    again_ref[1] = packed_ref[1]


def spread_kernel(own_ref, across_ref, passed_ref, copies_ref):
    other = [across_ref[n] + passed_ref[n] for n in range(2)]
    tiles = own_ref[0], other[0], own_ref[1] + other[1]
    for i in range(copies_ref.shape[0]):
        for n in range(3):
            copies_ref[i, n] = tiles[n]


def unpacker(own_ref, other_ref, odd_y, odd_x, slot, core=None):
    here = lax.axis_index("space")
    half_z = here // 8

    def moved(tile, by):
        if by & 1:
            tile = swap_x(tile, odd_x)
        if by & 2:
            tile = swap_y(tile, odd_y)
        return tile

    def unpack(i):
        tiles = [[None] * 8 for _ in range(3)]
        for j in range(4):
            for half in range(2):
                sent = []
                for g in range(4):
                    slab = 4 * g + j
                    at = i * 4 + (slab % 8) // 2, 2 if half else (slab // 8) ^ half_z
                    if core is None:
                        sent.append(jnp.where(here % 2 == slab % 2, own_ref[at], other_ref[at]))
                    else:
                        sent.append(own_ref[at] if core == slab % 2 else other_ref[at])
                for q in range(4 if half == 0 else 2):
                    place = slot ^ q
                    merged = jnp.where(
                        place == GRAY[0],
                        sent[0],
                        jnp.where(place == GRAY[1], sent[1], jnp.where(place == GRAY[2], sent[2], sent[3])),
                    )
                    plane = 4 * half + q
                    tiles[plane // 2][2 * j + plane % 2] = moved(merged, q)
        return tiles

    return unpack


def chain_step(flat, base, slot):
    now = [list(flat[8 * c : 8 * c + 8]) for c in range(3)]
    planes = [{k: now[c][k] for k in range(8)} for c in range(3)]
    for c in range(3):
        top = now[c][0]
        planes[c][8] = jnp.where(
            slot == GRAY[0],
            at_x(top, 1),
            jnp.where(slot == GRAY[1], at_y(top, 1), jnp.where(slot == GRAY[2], at_x(top, -1), 0.0)),
        )
        low = now[c][7]
        planes[c][-1] = jnp.where(
            slot == GRAY[1],
            at_x(low, -1),
            jnp.where(slot == GRAY[2], at_y(low, -1), jnp.where(slot == GRAY[3], at_x(low, 1), 0.0)),
        )
    spread = STEP * VISCOSITY / 4.0
    after = []
    vel = [[(STEP * 0.25) * planes[c][k] for k in range(8)] for c in range(3)]
    for c in range(3):
        for k in range(8):
            middle, upper, lower = planes[c][k], planes[c][k + 1], planes[c][k - 1]
            north, south = at_y(middle, 2), at_y(middle, -2)
            east, west = at_x(middle, 2), at_x(middle, -2)
            around = (upper + lower) + (north + south) + (east + west)
            advect = vel[0][k] * (east - west) + vel[1][k] * (north - south) + vel[2][k] * (upper - lower)
            after.append((base[c][k] + (1.0 - 6.0 * spread) * middle) + (spread * around - advect))
    return tuple(after)


def flat_tiles(tiles):
    return tuple(tile for row in tiles for tile in row)


def unpack_kernel(count, own_ref, other_ref, base_ref):
    row, col = parities()
    unpack = unpacker(own_ref, other_ref, row == 1, col == 1, row * 2 + col)
    for i in range(count):
        for n, tile in enumerate(flat_tiles(unpack(i))):
            base_ref[i, n] = tile


def stored(base_ref, i):
    return [[base_ref[i, 8 * c + k] for k in range(8)] for c in range(3)]


def runs_wave(wave, count):
    slice_id = lax.axis_index("tm")
    runs = (slice_id // count == wave) & (lax.axis_index("space") % 2 == 0)
    return runs if wave == GROUPS - 2 else runs & (slice_id % count >= count // 2)


def first_wave_kernel(count, own_ref, other_ref, out_ref):
    row, col = parities()
    slot = row * 2 + col
    unpack = unpacker(own_ref, other_ref, row == 1, col == 1, slot, 0)

    @pl.when(runs_wave(0, count))
    def _():
        state = flat_tiles(unpack(0))
        for i in range(1, count):
            state = chain_step(state, unpack(i), slot)
        for n in range(24):
            out_ref[n] = state[n]


def wave_kernel(wave, count, base_ref, state_ref, out_ref):
    row, col = parities()
    slot = row * 2 + col

    @pl.when(runs_wave(wave, count))
    def _():
        state = tuple(state_ref[n] for n in range(24))
        for i in range(count):
            state = chain_step(state, stored(base_ref, i), slot)
        for n in range(24):
            out_ref[n] = state[n]


def last_kernel(
    count, base_ref, state_ref, given_ref, late_ref, nodes_ref, mid_ref, end_ref, prev_ref, edge_ref,
    start_c_ref, end_c_ref, out_ref, states,
):
    here = lax.axis_index("space")
    slice_id = lax.axis_index("tm")
    row, col = parities()
    odd_y, odd_x = row == 1, col == 1
    slot = row * 2 + col
    own = slice_id % count
    in_first = slice_id // count == 0
    is_last = slice_id // count == GROUPS - 1
    at_corner = functools.reduce(operator.or_, [slice_id == i for i in CORNERS])

    def keep(i, flat):
        for n in range(24):
            states[i, n] = flat[n]

    from_own = here % 2 == 0
    state = tuple(
        jnp.where(from_own, state_ref[n], jnp.where(is_last, late_ref[n], given_ref[n])) for n in range(24)
    )
    keep(0, state)
    for i in range(count):
        base = stored(base_ref, i)
        state = chain_step(state, base, slot)
        if i == 0:
            state = tuple(jnp.where(in_first, b, after) for b, after in zip(flat_tiles(base), state))
        keep(i + 1, state)

    group = here // 4
    code = group ^ (group >> 1)
    own_y, own_x = code >> 1, code & 1
    base_k = 2 * (here % 4)

    def spread(tile):
        tile = jnp.where(row == own_y, tile, swap_y(tile, odd_y))
        return jnp.where(col == own_x, tile, swap_x(tile, odd_x))

    is_first = slice_id == 0
    for c in range(3):
        for k in range(2):
            w_end = spread(states[own + 1, 8 * c + base_k + k])
            v_start = start_c_ref[c, k]
            w_start = jnp.where(is_first, v_start, spread(states[own, 8 * c + base_k + k]))
            delta_start = w_start - v_start
            delta_end = w_end - end_c_ref[c, k]
            half = 0.5 * (delta_start + delta_end)
            handed = [jnp.where(at_corner, edge_ref[c, 2 * k + i], prev_ref[c, 2 * k + i]) for i in range(2)]
            delta_prev = w_start - restrict_pair(handed[0], handed[1], odd_y, odd_x)
            for i in range(2):
                z = 2 * k + i
                out_ref[0, 0, c, z] = jnp.where(is_first, nodes_ref[0, c, z], handed[i] + delta_prev)
                out_ref[0, 1, c, z] = mid_ref[c, z] + half
                out_ref[0, 2, c, z] = end_ref[c, z] + delta_end


def vmem(count):
    return [pl.BlockSpec(memory_space=pltpu.VMEM)] * count


def local(u_nodes):
    nodes = u_nodes[0]
    depth = nodes.shape[2]
    slabs = lax.axis_size("space")
    slices = lax.axis_size("tm")
    tile = nodes.shape[3:]
    shape = lambda *lead: jax.ShapeDtypeStruct(lead + tile, jnp.float32)
    both = ("tm", "space")
    middle = slabs // 2
    even = lax.axis_index("space") % 2 == 0
    top, bottom = nodes[:, :, depth - WIDE :], nodes[:, :, :WIDE]

    def swaps(pairs):
        return [(i, j) for i, j in pairs] + [(j, i) for i, j in pairs]

    to_side = jnp.where(even, bottom, top)
    side = lax.ppermute(to_side, "space", swaps([(i, i + 1) for i in range(1, slabs - 1, 2)]))
    near = lax.ppermute(jnp.where(even, top, bottom), "space", swaps([(i, i + 1) for i in range(0, slabs, 2)]))
    mid, end, start_c, end_c, packed, again = pl.pallas_call(
        fine_kernel,
        out_shape=[shape(3, 4), shape(3, 4), shape(3, 2), shape(3, 2), shape(4), shape(2)],
        in_specs=vmem(3),
        out_specs=vmem(6),
        compiler_params=PARAMS,
        name="fine",
    )(near, side, nodes)
    across = lax.ppermute(packed, "space", [(i, (i + middle) % slabs) for i in range(1, slabs)])
    beside = lax.ppermute(again, "space", [(0, middle + 1)])
    passed = lax.ppermute(beside, "space", [(middle + 1, middle)])
    copies = pl.pallas_call(
        spread_kernel,
        out_shape=shape(32, 3),
        in_specs=vmem(3),
        out_specs=vmem(1)[0],
        compiler_params=PARAMS,
        name="spread",
    )(packed, across, passed)

    device = lambda zl, y, zh, x, core: (zl * 4 + y) * slabs + zh * 8 + x * 2 + core
    layers = [
        [device(2 * g + zl, y, zh, x, core) for zl in range(2) for y in range(4) for x in range(4)]
        for g in range(GROUPS)
        for zh in range(2)
        for core in range(2)
    ]
    own = lax.all_to_all(copies, both, 0, 0, axis_index_groups=layers)
    edge = lax.ppermute(end, "tm", [(i - 1, i) for i in CORNERS])
    own, edge = lax.optimization_barrier((own, edge))
    other = lax.ppermute(own, "space", swaps([(i, i + 1) for i in range(0, slabs, 2)]))
    count = slices // GROUPS

    def cores(groups, begin=0):
        return [((g * count + i) * slabs + s) for g in groups for i in range(begin, count) for s in range(0, slabs, 2)]

    def handed_on(after, wave):
        senders = cores([wave], count // 2)
        upper = lax.ppermute(after, both, [(i, i + count * slabs) for i in senders])
        lower = lax.ppermute(after, both, [(i, i + count // 2 * slabs) for i in senders])
        return upper, lower

    after = pl.pallas_call(
        functools.partial(first_wave_kernel, count),
        out_shape=shape(24),
        in_specs=vmem(2),
        out_specs=vmem(1)[0],
        compiler_params=PARAMS,
        name="wave",
    )(own, other)
    own, after = lax.optimization_barrier((own, after))
    bases = pl.pallas_call(
        functools.partial(unpack_kernel, count),
        out_shape=shape(count, 24),
        in_specs=vmem(2),
        out_specs=vmem(1)[0],
        compiler_params=PARAMS,
        cost_estimate=pl.CostEstimate(flops=10_000_000, bytes_accessed=10_000_000, transcendentals=0),
        name="unpack",
    )(own, other)
    upper, lower = handed_on(after, 0)
    state = lower + upper
    for wave in range(1, GROUPS - 1):
        after = pl.pallas_call(
            functools.partial(wave_kernel, wave, count),
            out_shape=shape(24),
            in_specs=vmem(2),
            out_specs=vmem(1)[0],
            compiler_params=PARAMS,
            name="wave",
        )(bases, state)
        early, after = lax.optimization_barrier((state, after))
        if wave == 1:
            handed, after = lax.optimization_barrier((end, after))
            prev = lax.ppermute(handed, "tm", [(i, i + 1) for i in range(slices - 1) if i + 1 not in CORNERS])
        if wave < GROUPS - 2:
            upper, lower = handed_on(after, wave)
            prev, lower, upper = lax.optimization_barrier((prev, lower, upper))
            state = lower + upper + early
        else:
            state = lax.ppermute(after, both, [(i, i + count * slabs) for i in cores([wave])]) + early
    late = lax.ppermute(after, both, [(i, i + count * slabs + 1) for i in cores([GROUPS - 2])])
    given = lax.ppermute(early, both, [(i, i + 1) for i in cores(range(1, GROUPS - 1))])
    return pl.pallas_call(
        functools.partial(last_kernel, count),
        out_shape=shape(1, 3, 3, 4),
        in_specs=vmem(11),
        out_specs=vmem(1)[0],
        scratch_shapes=[pltpu.VMEM((count + 1, 24) + tile, jnp.float32)],
        compiler_params=PARAMS,
        name="last",
    )(bases, state, given, late, nodes, mid, end, prev, edge, start_c, end_c)


def solution(mesh):
    return jax.shard_map(
        local,
        mesh=mesh,
        in_specs=(P("tm", None, None, "space", None, None),),
        out_specs=P("tm", None, None, "space", None, None),
        check_vma=False,
    )
```

```python
import functools
import operator

import jax
import jax.numpy as jnp
from jax import lax
from jax.experimental import pallas as pl
from jax.experimental.pallas import tpu as pltpu
from jax.sharding import PartitionSpec as P

STEP = 0.2
VISCOSITY = 0.1
FIRST_ROW = (5.0 / 24.0, 1.0 / 3.0, -1.0 / 24.0)
SECOND_ROW = (-1.0 / 24.0, 1.0 / 3.0, 5.0 / 24.0)

GRAY = (0, 1, 3, 2)
WIDE = 3
PARAMS = pltpu.CompilerParams(vmem_limit_bytes=24 * 1024 * 1024)
GROUPS = 4
CORNERS = (8, 12, 16, 24)


def at_x(tile, shift):
    return pltpu.roll(tile, (-shift) % 128, 1)


def at_y(tile, shift):
    return pltpu.roll(tile, (-shift) % 8, 0)


def parities():
    row = lax.broadcasted_iota(jnp.int32, (8, 128), 0) & 1
    col = lax.broadcasted_iota(jnp.int32, (8, 128), 1) & 1
    return row, col


def swap_x(tile, odd_x):
    return jnp.where(odd_x, at_x(tile, -1), at_x(tile, 1))


def swap_y(tile, odd_y):
    return jnp.where(odd_y, at_y(tile, -1), at_y(tile, 1))


def rates(vel, upper, middle, lower, spacing, stride):
    north, south = at_y(middle, stride), at_y(middle, -stride)
    east, west = at_x(middle, stride), at_x(middle, -stride)
    advect = vel[0] * (east - west) + vel[1] * (north - south) + vel[2] * (upper - lower)
    diffuse = (upper + lower) + (north + south) + (east + west) - 6.0 * middle
    return diffuse * (VISCOSITY / (spacing * spacing)) - advect * (0.5 / spacing)


def tendency(planes, low, high, spacing, stride):
    out = [{} for _ in range(3)]
    for z in range(low, high):
        vel = [planes[c][z] for c in range(3)]
        for c in range(3):
            out[c][z] = rates(vel, planes[c][z + 1], planes[c][z], planes[c][z - 1], spacing, stride)
    return out


def restrict_pair(first, second, odd_y, odd_x):
    total = first + second
    total = total + swap_y(total, odd_y)
    total = total + swap_x(total, odd_x)
    return total * 0.125


def fine_kernel(near_ref, side_ref, nodes_ref, mid_ref, end_ref, start_c_ref, end_c_ref, packed_ref, again_ref):
    here = lax.axis_index("space")
    last = lax.axis_size("space") - 1
    even = here % 2 == 0
    is_first = lax.axis_index("tm") == 0
    row, col = parities()
    odd_y, odd_x = row == 1, col == 1
    keep_low = here > 0
    keep_high = here < last
    def load(node):
        planes = [{} for _ in range(3)]
        for c in range(3):
            for z in range(-3, 7):
                if z < 0:
                    at = node, c, z + WIDE
                    planes[c][z] = jnp.where(even, side_ref[at], near_ref[at])
                elif z < 4:
                    planes[c][z] = nodes_ref[node, c, z]
                else:
                    at = node, c, z - 4
                    planes[c][z] = jnp.where(even, near_ref[at], side_ref[at])
        return planes

    def inside(tile, z):
        if z < 0:
            return jnp.where(keep_low, tile, 0.0)
        if z > 3:
            return jnp.where(keep_high, tile, 0.0)
        return tile

    start = load(0)
    f0 = tendency(start, -2, 6, 1.0, 1)
    f1 = tendency(load(1), -2, 6, 1.0, 1)
    f2 = tendency(load(2), -2, 6, 1.0, 1)
    mid = [{} for _ in range(3)]
    for c in range(3):
        for z in range(-2, 6):
            value = start[c][z] + STEP * (
                FIRST_ROW[0] * f0[c][z] + FIRST_ROW[1] * f1[c][z] + FIRST_ROW[2] * f2[c][z]
            )
            mid[c][z] = inside(value, z)
    f_mid = tendency(mid, -1, 5, 1.0, 1)
    end = [{} for _ in range(3)]
    for c in range(3):
        for z in range(-1, 5):
            value = mid[c][z] + (
                0.5 * STEP * (f_mid[c][z] - f1[c][z])
                + STEP * (SECOND_ROW[0] * f0[c][z] + SECOND_ROW[1] * f1[c][z] + SECOND_ROW[2] * f2[c][z])
            )
            end[c][z] = inside(value, z)
    f_end = tendency(end, 0, 4, 1.0, 1)
    coarse = [
        {k: restrict_pair(start[c][2 * k], start[c][2 * k + 1], odd_y, odd_x) for k in range(-1, 3)} for c in range(3)
    ]
    h_start = tendency(coarse, 0, 2, 2.0, 2)
    planes = []
    for c in range(3):
        for z in range(4):
            mid_ref[c, z] = mid[c][z]
            end_ref[c, z] = end[c][z]
        for k in range(2):
            start_c_ref[c, k] = coarse[c][k]
            end_c_ref[c, k] = restrict_pair(end[c][2 * k], end[c][2 * k + 1], odd_y, odd_x)
            integral = [
                STEP * (f0[c][z] / 6.0 + (2.0 / 3.0) * f_mid[c][z] + f_end[c][z] / 6.0) for z in (2 * k, 2 * k + 1)
            ]
            base = restrict_pair(integral[0], integral[1], odd_y, odd_x) - STEP * h_start[c][k]
            first_end = coarse[c][k] + (STEP * h_start[c][k] + base)
            planes.append(jnp.where(is_first, first_end, base))
    group = here // 4
    own = group ^ (group >> 1)
    place = (row * 2 + col) ^ own
    packed_ref[0] = jnp.where(
        place == 0, planes[0], jnp.where(place == 1, planes[1], jnp.where(place == 2, planes[2], planes[3]))
    )
    packed_ref[1] = jnp.where(place == 0, planes[4], jnp.where(place == 1, planes[5], 0.0))
    for n in range(2, packed_ref.shape[0]):
        packed_ref[n] = jnp.zeros((8, 128), jnp.float32)
    again_ref[0] = packed_ref[0]
    again_ref[1] = packed_ref[1]


def spread_kernel(own_ref, across_ref, passed_ref, copies_ref):
    other = [across_ref[n] + passed_ref[n] for n in range(2)]
    tiles = own_ref[0], other[0], own_ref[1] + other[1]
    for i in range(copies_ref.shape[0]):
        for n in range(3):
            copies_ref[i, n] = tiles[n]


def unpacker(own_ref, other_ref, odd_y, odd_x, slot, core=None):
    here = lax.axis_index("space")
    half_z = here // 8

    def moved(tile, by):
        if by & 1:
            tile = swap_x(tile, odd_x)
        if by & 2:
            tile = swap_y(tile, odd_y)
        return tile

    def unpack(i):
        tiles = [[None] * 8 for _ in range(3)]
        for j in range(4):
            for half in range(2):
                sent = []
                for g in range(4):
                    slab = 4 * g + j
                    at = (slab % 8) // 2 * 8 + i, 2 if half else (slab // 8) ^ half_z
                    if core is None:
                        sent.append(jnp.where(here % 2 == slab % 2, own_ref[at], other_ref[at]))
                    else:
                        sent.append(own_ref[at] if core == slab % 2 else other_ref[at])
                for q in range(4 if half == 0 else 2):
                    place = slot ^ q
                    merged = jnp.where(
                        place == GRAY[0],
                        sent[0],
                        jnp.where(place == GRAY[1], sent[1], jnp.where(place == GRAY[2], sent[2], sent[3])),
                    )
                    plane = 4 * half + q
                    tiles[plane // 2][2 * j + plane % 2] = moved(merged, q)
        return tiles

    return unpack


def chain_step(flat, base, slot):
    now = [list(flat[8 * c : 8 * c + 8]) for c in range(3)]
    planes = [{k: now[c][k] for k in range(8)} for c in range(3)]
    for c in range(3):
        top = now[c][0]
        planes[c][8] = jnp.where(
            slot == GRAY[0],
            at_x(top, 1),
            jnp.where(slot == GRAY[1], at_y(top, 1), jnp.where(slot == GRAY[2], at_x(top, -1), 0.0)),
        )
        low = now[c][7]
        planes[c][-1] = jnp.where(
            slot == GRAY[1],
            at_x(low, -1),
            jnp.where(slot == GRAY[2], at_y(low, -1), jnp.where(slot == GRAY[3], at_x(low, 1), 0.0)),
        )
    spread = STEP * VISCOSITY / 4.0
    after = []
    vel = [[(STEP * 0.25) * planes[c][k] for k in range(8)] for c in range(3)]
    for c in range(3):
        for k in range(8):
            middle, upper, lower = planes[c][k], planes[c][k + 1], planes[c][k - 1]
            north, south = at_y(middle, 2), at_y(middle, -2)
            east, west = at_x(middle, 2), at_x(middle, -2)
            around = (upper + lower) + (north + south) + (east + west)
            advect = vel[0][k] * (east - west) + vel[1][k] * (north - south) + vel[2][k] * (upper - lower)
            after.append((base[c][k] + (1.0 - 6.0 * spread) * middle) + (spread * around - advect))
    return tuple(after)


def flat_tiles(tiles):
    return tuple(tile for row in tiles for tile in row)


def unpack_kernel(count, own_ref, other_ref, base_ref):
    row, col = parities()
    unpack = unpacker(own_ref, other_ref, row == 1, col == 1, row * 2 + col)
    for i in range(count):
        for n, tile in enumerate(flat_tiles(unpack(i))):
            base_ref[i, n] = tile


def stored(base_ref, i):
    return [[base_ref[i, 8 * c + k] for k in range(8)] for c in range(3)]


def runs_wave(wave, count):
    return (lax.axis_index("tm") // count == wave) & (lax.axis_index("space") % 2 == 0)


def first_wave_kernel(count, own_ref, other_ref, out_ref):
    row, col = parities()
    slot = row * 2 + col
    unpack = unpacker(own_ref, other_ref, row == 1, col == 1, slot, 0)

    @pl.when(runs_wave(0, count))
    def _():
        state = flat_tiles(unpack(0))
        for i in range(1, count):
            state = chain_step(state, unpack(i), slot)
        for n in range(24):
            out_ref[n] = state[n]


def wave_kernel(wave, count, base_ref, state_ref, out_ref):
    row, col = parities()
    slot = row * 2 + col

    @pl.when(runs_wave(wave, count))
    def _():
        state = tuple(state_ref[n] for n in range(24))
        for i in range(count):
            state = chain_step(state, stored(base_ref, i), slot)
        for n in range(24):
            out_ref[n] = state[n]


def last_kernel(
    count, base_ref, state_ref, given_ref, late_ref, nodes_ref, mid_ref, end_ref, prev_ref, edge_ref,
    start_c_ref, end_c_ref, out_ref, states,
):
    here = lax.axis_index("space")
    slice_id = lax.axis_index("tm")
    row, col = parities()
    odd_y, odd_x = row == 1, col == 1
    slot = row * 2 + col
    own = slice_id % count
    in_first = slice_id // count == 0
    is_last = slice_id // count == GROUPS - 1
    at_corner = functools.reduce(operator.or_, [slice_id == i for i in CORNERS])

    def keep(i, flat):
        for n in range(24):
            states[i, n] = flat[n]

    from_own = here % 2 == 0
    state = tuple(
        jnp.where(from_own, state_ref[n], jnp.where(is_last, late_ref[n], given_ref[n])) for n in range(24)
    )
    keep(0, state)
    for i in range(count):
        base = stored(base_ref, i)
        state = chain_step(state, base, slot)
        if i == 0:
            state = tuple(jnp.where(in_first, b, after) for b, after in zip(flat_tiles(base), state))
        keep(i + 1, state)

    group = here // 4
    code = group ^ (group >> 1)
    own_y, own_x = code >> 1, code & 1
    base_k = 2 * (here % 4)

    def spread(tile):
        tile = jnp.where(row == own_y, tile, swap_y(tile, odd_y))
        return jnp.where(col == own_x, tile, swap_x(tile, odd_x))

    is_first = slice_id == 0
    for c in range(3):
        for k in range(2):
            w_end = spread(states[own + 1, 8 * c + base_k + k])
            v_start = start_c_ref[c, k]
            w_start = jnp.where(is_first, v_start, spread(states[own, 8 * c + base_k + k]))
            delta_start = w_start - v_start
            delta_end = w_end - end_c_ref[c, k]
            half = 0.5 * (delta_start + delta_end)
            handed = [jnp.where(at_corner, edge_ref[c, 2 * k + i], prev_ref[c, 2 * k + i]) for i in range(2)]
            delta_prev = w_start - restrict_pair(handed[0], handed[1], odd_y, odd_x)
            for i in range(2):
                z = 2 * k + i
                out_ref[0, 0, c, z] = jnp.where(is_first, nodes_ref[0, c, z], handed[i] + delta_prev)
                out_ref[0, 1, c, z] = mid_ref[c, z] + half
                out_ref[0, 2, c, z] = end_ref[c, z] + delta_end


def vmem(count):
    return [pl.BlockSpec(memory_space=pltpu.VMEM)] * count


def local(u_nodes):
    nodes = u_nodes[0]
    depth = nodes.shape[2]
    slabs = lax.axis_size("space")
    slices = lax.axis_size("tm")
    tile = nodes.shape[3:]
    shape = lambda *lead: jax.ShapeDtypeStruct(lead + tile, jnp.float32)
    both = ("tm", "space")
    middle = slabs // 2
    even = lax.axis_index("space") % 2 == 0
    top, bottom = nodes[:, :, depth - WIDE :], nodes[:, :, :WIDE]

    def swaps(pairs):
        return [(i, j) for i, j in pairs] + [(j, i) for i, j in pairs]

    to_side = jnp.where(even, bottom, top)
    side = lax.ppermute(to_side, "space", swaps([(i, i + 1) for i in range(1, slabs - 1, 2)]))
    near = lax.ppermute(jnp.where(even, top, bottom), "space", swaps([(i, i + 1) for i in range(0, slabs, 2)]))
    mid, end, start_c, end_c, packed, again = pl.pallas_call(
        fine_kernel,
        out_shape=[shape(3, 4), shape(3, 4), shape(3, 2), shape(3, 2), shape(4), shape(2)],
        in_specs=vmem(3),
        out_specs=vmem(6),
        compiler_params=PARAMS,
        name="fine",
    )(near, side, nodes)
    across = lax.ppermute(packed, "space", [(i, (i + middle) % slabs) for i in range(1, slabs)])
    beside = lax.ppermute(again, "space", [(0, middle + 1)])
    passed = lax.ppermute(beside, "space", [(middle + 1, middle)])
    copies = pl.pallas_call(
        spread_kernel,
        out_shape=shape(32, 3),
        in_specs=vmem(3),
        out_specs=vmem(1)[0],
        compiler_params=PARAMS,
        name="spread",
    )(packed, across, passed)

    device = lambda zl, y, zh, x, core: (zl * 4 + y) * slabs + zh * 8 + x * 2 + core
    layers = [
        [device(2 * g + zl, y, zh, x, core) for x in range(4) for zl in range(2) for y in range(4)]
        for g in range(GROUPS)
        for zh in range(2)
        for core in range(2)
    ]
    own = lax.all_to_all(copies, both, 0, 0, axis_index_groups=layers)
    edge = lax.ppermute(end, "tm", [(i - 1, i) for i in CORNERS])
    own, edge = lax.optimization_barrier((own, edge))
    other = lax.ppermute(own, "space", swaps([(i, i + 1) for i in range(0, slabs, 2)]))
    count = slices // GROUPS

    def cores(groups):
        return [((g * count + i) * slabs + s) for g in groups for i in range(count) for s in range(0, slabs, 2)]

    after = pl.pallas_call(
        functools.partial(first_wave_kernel, count),
        out_shape=shape(24),
        in_specs=vmem(2),
        out_specs=vmem(1)[0],
        compiler_params=PARAMS,
        name="wave",
    )(own, other)
    own, after = lax.optimization_barrier((own, after))
    bases = pl.pallas_call(
        functools.partial(unpack_kernel, count),
        out_shape=shape(count, 24),
        in_specs=vmem(2),
        out_specs=vmem(1)[0],
        compiler_params=PARAMS,
        cost_estimate=pl.CostEstimate(flops=10_000_000, bytes_accessed=10_000_000, transcendentals=0),
        name="unpack",
    )(own, other)
    state = lax.ppermute(after, both, [(i, i + count * slabs) for i in cores([0])])
    for wave in range(1, GROUPS - 1):
        after = pl.pallas_call(
            functools.partial(wave_kernel, wave, count),
            out_shape=shape(24),
            in_specs=vmem(2),
            out_specs=vmem(1)[0],
            compiler_params=PARAMS,
            name="wave",
        )(bases, state)
        early, after = lax.optimization_barrier((state, after))
        if wave == 1:
            handed, after = lax.optimization_barrier((end, after))
            prev = lax.ppermute(handed, "tm", [(i, i + 1) for i in range(slices - 1) if i + 1 not in CORNERS])
        moved = lax.ppermute(after, both, [(i, i + count * slabs) for i in cores([wave])])
        if wave == 1:
            prev, moved = lax.optimization_barrier((prev, moved))
        state = moved + early
    late = lax.ppermute(after, both, [(i, i + count * slabs + 1) for i in cores([GROUPS - 2])])
    given = lax.ppermute(early, both, [(i, i + 1) for i in cores(range(1, GROUPS - 1))])
    return pl.pallas_call(
        functools.partial(last_kernel, count),
        out_shape=shape(1, 3, 3, 4),
        in_specs=vmem(11),
        out_specs=vmem(1)[0],
        scratch_shapes=[pltpu.VMEM((count + 1, 24) + tile, jnp.float32)],
        compiler_params=PARAMS,
        name="last",
    )(bases, state, given, late, nodes, mid, end, prev, edge, start_c, end_c)


def solution(mesh):
    return jax.shard_map(
        local,
        mesh=mesh,
        in_specs=(P("tm", None, None, "space", None, None),),
        out_specs=P("tm", None, None, "space", None, None),
        check_vma=False,
    )
```
